128 devices in a mesh: visit: 8 (over x, core), tile: 16 (over y, z).
Axes of the slice: x: 4, y: 4, z: 4, core: 2. Of those that a mesh axis runs over, the one named last changes fastest.
Arguments:
- image: bfloat16 [1536, 512, 512], P(('visit', 'tile')), may hold values from -6 to 6
- inv_var: bfloat16 [1536, 512], P(('visit', 'tile')), may hold values from 0.099609375 to 3
- kernel_index: int32 [1536], P(('visit', 'tile')), may hold values from 0 to 7
- dest: int32 [1536, 1], P(('visit', 'tile')), may hold values from 0 to 15; in each aligned block of 12 rows (0 to 11, 12 to 23, ...) at most 2 rows name the same one
- position: int32 [1536], P(('visit', 'tile')), may hold values from 0 to 3
- row_taps: float32 [8, 41], replicated, may hold values from 0.005 to 0.06
- col_taps: float32 [8, 41], replicated, may hold values from 0.005 to 0.06
Outputs:
- coadd: float32 [16, 4, 512, 512], P('tile', None, 'visit')
The draws below stay inside these ranges and needn't reach their ends.
Inputs may be any that keep to these rules, and one draw needn't show every extreme that they name: `dest`: among the rows of one device no sky tile is named more than 2 times.
All inputs are finite; a program needn't handle non-finite values.
Results may differ from the reference program's by a relative error of at most 0.0055.
Values may be sent and summed in bfloat16 or wider, within the bound.
No kernel may reach another device: no remote copies, remote signals or barrier semaphores. Data moves between devices by JAX's collectives and lax.ppermute only.
A program may use at most 192 MiB of HBM per device.

```python
import math
import jax
import jax.numpy as jnp
import numpy as np
from jax import lax

B = 512
TAPS = 41
NB = 8
POS = 4
CAP = 2
BLK_DEV = 12
BLOCKS = 1536
SKY_TILES = 16
N_TILE = 16


def with_ends(values, stream_key, low, high):
    place = [jax.random.randint(jax.random.fold_in(stream_key, axis), (), 0, length) for axis, length in enumerate(values.shape)]
    longest = values.shape.index(max(values.shape))
    beside = place[:longest] + [(place[longest] + 1) % values.shape[longest]] + place[longest + 1:]
    return values.at[tuple(place)].set(low).at[tuple(beside)].set(high)


def level_of(stream_key, extent, pieces, low, top_value):
    def one(dim, blocks):
        steps = jax.random.uniform(jax.random.fold_in(jax.random.fold_in(stream_key, 6), dim), (blocks,), jnp.float32, low / len(pieces), top_value / len(pieces))
        return jnp.repeat(jnp.exp(steps), extent[dim] // blocks).reshape((-1,) + (1,) * (len(extent) - dim - 1))

    level = one(*pieces[0])
    for cut in pieces[1:]:
        level = level * one(*cut)
    return level


def assign_block(rng, own, number, rows, number_of, top, bound, slope):
    ranking = jax.random.permutation(rng, number_of)
    crowded, common = shares(number_of, rows * top, bound, slope, True), shares(number_of, rows * top, bound, slope, False)
    places = jnp.arange(number_of)

    def named(lengths, offset_by):
        used = int((lengths > 0).sum())
        fixed = max(1, used // 4)
        moved = fixed + (places - fixed + offset_by * (used - fixed)) % max(1, number_of - fixed)
        return jnp.zeros((number_of,), jnp.int32).at[ranking[jnp.where(places < fixed, places, moved)]].set(jnp.asarray(lengths, jnp.int32))

    lengths = jnp.where(number % 4 == 0, named(crowded, number // 4), named(common, number - number // 4 - 1))
    mixed = jax.random.permutation(jax.random.fold_in(own, 3), number_of)
    donor, taker = mixed[0:number_of // 2 * 2:2], mixed[1:number_of // 2 * 2:2]
    margin = jnp.minimum(lengths[donor] - 1, bound - lengths[taker]) // 2
    margin = jnp.where((donor == ranking[0]) | (taker == ranking[0]) | (lengths[taker] == 0), 0, jnp.maximum(margin, 0))
    moved = jax.random.randint(jax.random.fold_in(own, 4), (number_of // 2,), 0, 1 << 20) % (margin + 1)
    lengths = lengths.at[donor].add(-moved).at[taker].add(moved)
    labels = jnp.searchsorted(jnp.cumsum(lengths), jnp.arange(rows * top), side="right").astype(jnp.int32)
    listing = labels.reshape(top, rows).T
    listing = listing[jax.random.permutation(jax.random.fold_in(own, 1), rows)]
    offset_by = jax.random.randint(jax.random.fold_in(own, 2), (rows, 1), 0, top)
    return jnp.take_along_axis(listing, (jnp.arange(top)[None, :] + offset_by) % top, axis=1)


def shares(amount, total, reach, skew, full):
    weights = [(1 << 20) // math.isqrt(standing ** skew) + 1 for standing in range(1, amount + 1)]
    largest = reach if full else min(reach, max(-(-total // amount), total * weights[0] // sum(weights)))
    least = 1 if total - largest >= amount - 1 else 0
    holding, spare = [largest] + [least] * (amount - 1), total - largest - least * (amount - 1)
    while spare > 0:
        candidates = [i for i in range(1, amount) if holding[i] < largest] or [i for i in range(1, amount) if holding[i] < reach]
        mass, remaining = sum([weights[i] for i in candidates]), spare
        for i in candidates:
            more = min(reach - holding[i], max(1, remaining * weights[i] // mass), spare)
            holding[i] = holding[i] + more
            spare = spare - more
    return np.array(holding)


def noise(stream_key, shape, deviation, limit, pieces=(), held_as=jnp.bfloat16):
    factor_of = level_of(stream_key, shape, pieces, -0.22, 0.18) if pieces else 1.0
    result = jax.random.normal(stream_key, shape, jnp.float32) * deviation * factor_of
    return jnp.minimum(jnp.maximum(result, -limit), limit).astype(held_as)


def setup_inputs(seed: int = 0) -> dict:
    key_list = jax.random.split(jax.random.key(seed), 8)
    image = noise(key_list[0], (BLOCKS, B, B), 1.0, 6.0, ((0, 128),))
    inv_var = jnp.clip(jnp.exp(math.log(3.0) - 3.4051113 * jax.random.uniform(key_list[1], (BLOCKS, B), jnp.float32) ** level_of(key_list[1], (BLOCKS, B), ((0, 128),), -0.2, 0.2)), 0.099609375, 3.0).astype(jnp.bfloat16)
    kernel_index = with_ends(jax.random.randint(key_list[2], (BLOCKS,), 0, NB), jax.random.fold_in(key_list[2], 1), 0, NB - 1).astype(jnp.int32)
    dest_keys = jax.random.split(jax.random.fold_in(key_list[3], 1), BLOCKS // BLK_DEV)
    dest_turns = jax.random.permutation(jax.random.fold_in(key_list[3], 3), BLOCKS // BLK_DEV)
    dest = jax.vmap(lambda own, number: assign_block(jax.random.fold_in(key_list[3], 2), own, number, BLK_DEV, N_TILE, 1, CAP, 2))(dest_keys, dest_turns).reshape((BLOCKS, 1))
    position = with_ends(jax.random.randint(key_list[4], (BLOCKS,), 0, POS), jax.random.fold_in(key_list[4], 1), 0, POS - 1).astype(jnp.int32)
    row_taps = jnp.clip(jnp.exp(jax.random.uniform(key_list[5], (NB, TAPS), jnp.float32, math.log(0.005), math.log(0.06))), 0.005, 0.06)
    col_taps = jnp.clip(jnp.exp(jax.random.uniform(key_list[6], (NB, TAPS), jnp.float32, math.log(0.005), math.log(0.06))), 0.005, 0.06)
    return {"image": image, "inv_var": inv_var, "kernel_index": kernel_index, "dest": dest, "position": position, "row_taps": row_taps, "col_taps": col_taps}


def band_tables(tap_table, side_len):
    tap_count = tap_table.shape[1]
    rows_at = jnp.arange(side_len, dtype=jnp.int32)[:, None]
    cols_at = jnp.arange(side_len, dtype=jnp.int32)[None, :]
    offset = rows_at - cols_at + (tap_count - 1) // 2
    inside = (offset >= 0) & (offset < tap_count)
    picked = jnp.take(tap_table, jnp.clip(offset, 0, tap_count - 1), axis=1)
    return jnp.where(inside[None], picked, jnp.zeros_like(picked)).astype(jnp.bfloat16)


def reference(image, inv_var, kernel_index, dest, position, row_taps, col_taps):
    row_bands = band_tables(row_taps, B)
    col_bands = band_tables(col_taps, B)
    target = dest[:, 0].astype(jnp.int32)

    def absorb(carry, packed):
        numerator, denominator = carry
        pixels, weight, kernel_id, tile_id, pos_id = packed
        half_pass = jnp.dot(row_bands[kernel_id], pixels, preferred_element_type=jnp.float32).astype(jnp.bfloat16)
        matched = jnp.dot(half_pass, col_bands[kernel_id].T, preferred_element_type=jnp.float32).astype(jnp.bfloat16)
        weight_f = weight.astype(jnp.float32)
        contrib = weight_f[:, None] * matched.astype(jnp.float32)
        numerator = numerator.at[tile_id, pos_id].add(contrib)
        denominator = denominator.at[tile_id, pos_id].add(weight_f)
        return (numerator, denominator), None

    start = (jnp.zeros((SKY_TILES, POS, B, B), jnp.float32), jnp.zeros((SKY_TILES, POS, B), jnp.float32))
    (numerator, denominator), _ = lax.scan(absorb, start, (image, inv_var, kernel_index.astype(jnp.int32), target, position.astype(jnp.int32)))
    return numerator / jnp.maximum(denominator, 1.0)[..., None]
```

```python
import functools

import jax
import jax.numpy as jnp
from jax import lax
from jax.experimental import pallas as pl
from jax.experimental.pallas import tpu as pltpu
from jax.sharding import PartitionSpec as P

NB = 8
POS = 4
LANE = 128
BF = jnp.bfloat16
F32 = jnp.float32
CHUNKS = ((0, 128), (128, 128), (256, 128), (384, 128))


def toeplitz(row, length):
    wide = jnp.broadcast_to(row, (LANE, length))
    return pltpu.roll(wide, 0, 1, stride=1, stride_axis=0)


def match_kernel(col0, width, kidx_ref, rtap_ref, ctap_ref, img_ref, iv_ref, *rest):
    outs, (rband, cband, whole) = rest[:-3], rest[-3:]
    parts = len(outs)
    b = pl.program_id(0)
    side = img_ref.shape[2]
    blocks = iv_ref.shape[0]
    taps = rtap_ref.shape[1]
    half = (taps - 1) // 2
    length = 3 * LANE
    rows = side // parts

    @pl.when(b == 0)
    def _():
        q = lax.broadcasted_iota(jnp.int32, (taps, length), 0)
        n = lax.broadcasted_iota(jnp.int32, (taps, length), 1)
        pick = (n + q == LANE + half).astype(F32).astype(BF)
        rbase = jnp.dot(rtap_ref[...].astype(BF), pick, preferred_element_type=F32)
        cbase = jnp.dot(ctap_ref[...].astype(BF), pick, preferred_element_type=F32)
        rband[...] = jnp.zeros_like(rband)
        tiles = side // LANE
        for k in range(NB):
            t = toeplitz(rbase[k : k + 1], length).astype(BF)
            for a in range(tiles):
                lo, hi = max(a - 1, 0), min(a + 2, tiles)
                off = (lo - (a - 1)) * LANE
                rband[k, a * LANE : (a + 1) * LANE, lo * LANE : hi * LANE] = t[
                    :, off : off + (hi - lo) * LANE
                ]
            cband[k] = toeplitz(cbase[k : k + 1], length).astype(BF)

    k = kidx_ref[b]
    tiles = side // LANE
    pieces = []
    for g in range(col0 // LANE, (col0 + width) // LANE):
        lo, hi = max(g - 1, 0), min(g + 2, tiles)
        off = (lo - (g - 1)) * LANE
        window = img_ref[0, :, lo * LANE : hi * LANE]
        ct = cband[k, :, off : off + (hi - lo) * LANE]
        pieces.append(
            lax.dot_general(window, ct, (((1,), (1,)), ((), ())), preferred_element_type=F32).astype(BF)
        )
    mid = pieces[0] if len(pieces) == 1 else jnp.concatenate(pieces, axis=1)
    matched = jnp.dot(rband[k], mid, preferred_element_type=F32)
    onehot = (lax.broadcasted_iota(jnp.int32, (blocks, width), 0) == b).astype(F32).astype(BF)
    weight = lax.dot_general(iv_ref[...], onehot, (((0,), (0,)), ((), ())), preferred_element_type=F32)
    whole[...] = (matched * weight).astype(BF)
    me = lax.axis_index("visit")
    for i in range(parts):
        to = lax.rem(me + i, parts)
        outs[i][0] = whole[pl.ds(pl.multiple_of(to * rows, rows), rows), :]


def match_chunk(col0, width, parts, kidx, row_taps, col_taps, image, inv_var):
    blocks, side, _ = image.shape
    rows = side // parts
    length = 3 * LANE
    full = lambda shape: pl.BlockSpec(shape, lambda b, *_: (0,) * len(shape))
    grid_spec = pltpu.PrefetchScalarGridSpec(
        num_scalar_prefetch=1,
        grid=(blocks,),
        in_specs=[
            full(row_taps.shape),
            full(col_taps.shape),
            pl.BlockSpec((1, side, side), lambda b, *_: (b, 0, 0)),
            full(inv_var.shape),
        ],
        out_specs=[pl.BlockSpec((1, rows, width), lambda b, *_: (b, 0, 0))] * parts,
        scratch_shapes=[
            pltpu.VMEM((NB, side, side), BF),
            pltpu.VMEM((NB, LANE, length), BF),
            pltpu.VMEM((side, width), BF),
        ],
    )
    return pl.pallas_call(
        functools.partial(match_kernel, col0, width),
        grid_spec=grid_spec,
        out_shape=[jax.ShapeDtypeStruct((blocks, rows, width), BF)] * parts,
        compiler_params=pltpu.CompilerParams(vmem_limit_bytes=32 << 20),
        cost_estimate=pl.CostEstimate(
            flops=2 * blocks * side * side * 256 * 2,
            bytes_accessed=image.size * 2 + blocks * side * width * 2,
            transcendentals=0,
        ),
        name="match",
    )(kidx, row_taps, col_taps, image, inv_var)


def gather_kernel(combo_ref, *rest):
    parts = len(rest) - 2
    pieces, out_ref, acc = rest[:parts], rest[parts], rest[parts + 1]
    blocks = pieces[0].shape[0]
    me = lax.axis_index("visit")
    acc[...] = jnp.zeros_like(acc)
    for i in range(parts):
        base = lax.rem(me - i + parts, parts) * blocks
        for b in range(blocks):
            c = combo_ref[base + b]
            acc[c] += pieces[i][b].astype(F32)
    out_ref[...] = acc[...].astype(BF)


def gather_chunk(combos, pieces, count):
    blocks, rows, width = pieces[0].shape
    vm = pl.BlockSpec(memory_space=pltpu.VMEM)
    return pl.pallas_call(
        gather_kernel,
        in_specs=[pl.BlockSpec(memory_space=pltpu.SMEM)] + [vm] * len(pieces),
        out_specs=vm,
        out_shape=jax.ShapeDtypeStruct((count, rows, width), BF),
        scratch_shapes=[pltpu.VMEM((count, rows, width), F32)],
        compiler_params=pltpu.CompilerParams(vmem_limit_bytes=32 << 20),
        cost_estimate=pl.CostEstimate(
            flops=blocks * len(pieces) * rows * width * 2,
            bytes_accessed=blocks * len(pieces) * rows * width * 2 * 4,
            transcendentals=0,
        ),
        name="gather",
    )(combos, *pieces)


def per_device(image, inv_var, kernel_index, dest, position, row_taps, col_taps):
    tiles = lax.axis_size("tile")
    visits = lax.axis_size("visit")
    blocks, side, _ = image.shape
    rows = side // visits
    count = tiles * POS

    combo = dest[:, 0] * POS + position
    packed = jnp.concatenate(
        [inv_var, jnp.broadcast_to(combo.astype(BF)[:, None], (blocks, LANE))], axis=1
    )
    gathered = lax.all_gather(packed, "visit", axis=0, tiled=True)
    combos = gathered[:, side].astype(jnp.int32)
    me = lax.axis_index("visit")
    iv_rows = lax.dynamic_slice_in_dim(gathered, me * rows, rows, axis=1)
    table = (lax.broadcasted_iota(jnp.int32, (count, visits * blocks), 0) == combos[None, :]).astype(BF)
    den_part = jnp.dot(table, iv_rows, preferred_element_type=F32)
    den_all = lax.all_to_all(den_part.reshape(tiles, POS, rows), "tile", 0, 0, tiled=True)
    den = jnp.maximum(jnp.sum(den_all, axis=0), 1.0)

    results = []
    for col0, width in CHUNKS:
        pieces = match_chunk(col0, width, visits, kernel_index, row_taps, col_taps, image, inv_var)
        arrived = [pieces[0]]
        for i in range(1, visits):
            perm = [(s, (s + i) % visits) for s in range(visits)]
            arrived.append(lax.ppermute(pieces[i], "visit", perm))
        partial = gather_chunk(combos, arrived, count)
        swapped = lax.all_to_all(partial.reshape(tiles, POS * rows, width), "tile", 0, 0, tiled=True)
        total = jnp.sum(swapped.reshape(tiles, POS, rows, width).astype(F32), axis=0)
        results.append(total / den[:, :, None])
    return jnp.concatenate(results, axis=2)[None]


def solution(mesh):
    in_specs = (
        P(("visit", "tile"), None, None),
        P(("visit", "tile"), None),
        P(("visit", "tile")),
        P(("visit", "tile"), None),
        P(("visit", "tile")),
        P(),
        P(),
    )
    out_specs = P("tile", None, "visit", None)
    return jax.shard_map(
        per_device, mesh=mesh, in_specs=in_specs, out_specs=out_specs, check_vma=False
    )
```

```python
import functools

import jax
import jax.numpy as jnp
import numpy as np
from jax import lax
from jax.experimental import pallas as pl
from jax.experimental.pallas import tpu as pltpu
from jax.sharding import Mesh, PartitionSpec as P

NB = 8
POS = 4
LANE = 128
BF = jnp.bfloat16
F32 = jnp.float32
NX, NC, NY, NZ = 4, 2, 4, 4
VISITS, TILES = NX * NC, NY * NZ
COUNT = TILES * POS
SUB = 16
VMEM_BIG = 60 << 20
Y_OFFSETS = tuple((dc, dy) for dc in range(NC) for dy in range(NY))


def toeplitz(row, length):
    wide = jnp.broadcast_to(row, (LANE, length))
    return pltpu.roll(wide, 0, 1, stride=1, stride_axis=0)


def band_blocks(table, taps_ref):
    count = taps_ref.shape[1]
    half = (count - 1) // 2
    length = 3 * LANE
    q = lax.broadcasted_iota(jnp.int32, (count, length), 0)
    n = lax.broadcasted_iota(jnp.int32, (count, length), 1)
    pick = (n + q == LANE + half).astype(F32).astype(BF)
    base = jnp.dot(taps_ref[...].astype(BF), pick, preferred_element_type=F32)
    for k in range(NB):
        table[k] = toeplitz(base[k : k + 1], length).astype(BF)


def put_band(band, block, first, tiles):
    for a in range(band.shape[0] // LANE):
        at = first + a
        lo, hi = max(at - 1, 0), min(at + 2, tiles)
        off = (lo - (at - 1)) * LANE
        band[a * LANE : (a + 1) * LANE, lo * LANE : hi * LANE] = block[:, off : off + (hi - lo) * LANE]


def column_pass(b, h, mid, cband, iv_ref):
    blocks, side = iv_ref.shape
    width = side // 2
    onehot = (lax.broadcasted_iota(jnp.int32, (blocks, LANE), 0) == b).astype(F32).astype(BF)
    weight = lax.dot_general(iv_ref[...], onehot, (((0,), (0,)), ((), ())), preferred_element_type=F32)
    weight = jnp.concatenate([weight] * (width // LANE), axis=1)
    lo, hi = (0, 3 * LANE) if h == 0 else (side - 3 * LANE, side)
    matched = lax.dot_general(
        mid[:, lo:hi], cband[:, lo:hi], (((1,), (1,)), ((), ())), preferred_element_type=F32
    )
    return (matched * weight).astype(BF)


def combo_rows(dest_ref, pos_ref, blocks):
    row = lax.broadcasted_iota(jnp.int32, (SUB, LANE), 0)
    places = jnp.full((SUB, LANE), COUNT, jnp.int32)
    for b in range(blocks):
        places = jnp.where(row == b, dest_ref[b] * POS + pos_ref[b], places)
    return places.astype(F32).astype(BF)


def first_kernel(kidx_ref, dest_ref, pos_ref, rtap_ref, ctap_ref, img_ref, iv_ref, mid_ref, *rest):
    y_refs, (rtab, ctab, rband, cband, whole) = rest[:-5], rest[-5:]
    b = pl.program_id(0)
    blocks, side = iv_ref.shape
    tiles, rows = side // LANE, side // VISITS

    @pl.when(b == 0)
    def _():
        band_blocks(rtab, rtap_ref)
        band_blocks(ctab, ctap_ref)
        rband[...] = jnp.zeros_like(rband)
        cband[...] = jnp.zeros_like(cband)
        places = combo_rows(dest_ref, pos_ref, blocks)
        for ref in y_refs:
            ref[blocks * rows :, LANE:] = places
            ref[blocks * rows :, :LANE] = places

    k = kidx_ref[b]
    put_band(rband, rtab.at[k], 0, tiles)
    put_band(cband, ctab.at[k], tiles // 2, tiles)
    mid = jnp.dot(rband[...], img_ref[0], preferred_element_type=F32).astype(BF)
    mid_ref[0] = mid
    whole[...] = column_pass(b, 1, mid, cband, iv_ref)
    mc, my = lax.axis_index("core"), lax.axis_index("y")
    for i, (dc, dy) in enumerate(Y_OFFSETS):
        core, sub = lax.rem(mc + dc, NC), lax.rem(my + dy, NY)
        for x in range(NX):
            start = pl.multiple_of((x * NC + core) * rows + sub * SUB, SUB)
            to = pl.multiple_of(b * rows + x * SUB, SUB)
            y_refs[i][pl.ds(to, SUB), :] = whole[pl.ds(start, SUB), :]


def second_kernel(kidx_ref, dest_ref, pos_ref, ctap_ref, mid_ref, iv_ref, x_ref, ctab, cband):
    b = pl.program_id(0)
    blocks, side = iv_ref.shape
    tiles, rows = side // LANE, side // VISITS

    @pl.when(b == 0)
    def _():
        band_blocks(ctab, ctap_ref)
        cband[...] = jnp.zeros_like(cband)
        places = combo_rows(dest_ref, pos_ref, blocks)
        weights = jnp.concatenate([iv_ref[...].astype(F32), jnp.zeros((SUB - blocks, side), F32)], axis=0)
        for v in range(VISITS):
            part = weights[:, (v // 2) * LANE : (v // 2 + 1) * LANE]
            if v % 2:
                part = pltpu.roll(part, rows, 1)
            x_ref[v, blocks * rows :, :LANE] = part.astype(BF)
            x_ref[v, blocks * rows :, LANE:] = places

    put_band(cband, ctab.at[kidx_ref[b]], 0, tiles)
    weighted = column_pass(b, 0, mid_ref[0], cband, iv_ref)
    at = pl.ds(pl.multiple_of(b * rows, rows), rows)
    for v in range(VISITS):
        x_ref[v, at, :] = weighted[v * rows : (v + 1) * rows]


def match(kidx, dest, position, row_taps, col_taps, image, inv_var):
    blocks, side, _ = image.shape
    rows, width = side // VISITS, side // 2
    tall = blocks * rows + SUB
    full = lambda shape: pl.BlockSpec(shape, lambda b, *_: (0,) * len(shape))
    block = pl.BlockSpec((1, side, side), lambda b, *_: (b, 0, 0))
    table, half_band = pltpu.VMEM((NB, LANE, 3 * LANE), BF), pltpu.VMEM((width, side), BF)
    shape = jax.ShapeDtypeStruct
    params = pltpu.CompilerParams(vmem_limit_bytes=VMEM_BIG)
    mid, *y_parts = pl.pallas_call(
        first_kernel,
        grid_spec=pltpu.PrefetchScalarGridSpec(
            num_scalar_prefetch=3,
            grid=(blocks,),
            in_specs=[full(row_taps.shape), full(col_taps.shape), block, full(inv_var.shape)],
            out_specs=[block] + [full((tall, width))] * len(Y_OFFSETS),
            scratch_shapes=[table, table, pltpu.VMEM((side, side), BF), half_band, pltpu.VMEM((side, width), BF)],
        ),
        out_shape=[shape(image.shape, BF)] + [shape((tall, width), BF)] * len(Y_OFFSETS),
        compiler_params=params,
        cost_estimate=pl.CostEstimate(
            flops=3 * blocks * side**3, bytes_accessed=image.size * 5, transcendentals=0
        ),
        name="match_first",
    )(kidx, dest, position, row_taps, col_taps, image, inv_var)
    x_part = pl.pallas_call(
        second_kernel,
        grid_spec=pltpu.PrefetchScalarGridSpec(
            num_scalar_prefetch=3,
            grid=(blocks,),
            in_specs=[full(col_taps.shape), block, full(inv_var.shape)],
            out_specs=full((VISITS, tall, width)),
            scratch_shapes=[table, half_band],
        ),
        out_shape=shape((VISITS, tall, width), BF),
        compiler_params=params,
        cost_estimate=pl.CostEstimate(
            flops=blocks * side**3, bytes_accessed=image.size * 3, transcendentals=0
        ),
        name="match_second",
    )(kidx, dest, position, col_taps, mid, inv_var)
    return x_part, y_parts


def read_places(notes, flat, smem, sem):
    places = jnp.concatenate([n.astype(F32) for n in notes], axis=0)
    size = VISITS * SUB
    row = lax.broadcasted_iota(jnp.int32, (size, LANE), 0)
    lane = lax.broadcasted_iota(jnp.int32, (size, LANE), 1)
    line = jnp.sum(jnp.where(row == lane, places, 0.0), axis=0, keepdims=True)
    flat[...] = line.astype(jnp.int32)
    copy = pltpu.make_async_copy(flat, smem, sem)
    copy.start()
    copy.wait()
    return line


def gather_x_kernel(in_ref, after_ref, out_ref, acc, flat, smem, sem):
    rows, width = acc.shape[1:]
    blocks = (in_ref.shape[1] - SUB) // rows
    top = blocks * rows
    line = read_places([in_ref[v, top:, LANE:] for v in range(VISITS)], flat, smem, sem)
    acc[...] = jnp.zeros_like(acc)
    for v in range(VISITS):
        for b in range(blocks):
            acc[smem[0, v * SUB + b]] += in_ref[v, b * rows : (b + 1) * rows].astype(F32)
    place = lax.broadcasted_iota(jnp.int32, (COUNT, LANE), 0)
    hit = (place == line.astype(jnp.int32)).astype(F32).astype(BF)
    weights = jnp.concatenate([in_ref[v, top:, :LANE].astype(F32) for v in range(VISITS)], axis=0).astype(BF)
    den = jnp.dot(hit, weights, preferred_element_type=F32)
    high = den.astype(BF).astype(F32)
    both = jnp.concatenate([high, den - high], axis=1)
    for t in range(TILES):
        for p in range(POS):
            out_ref[t, p * rows : (p + 1) * rows] = acc[t * POS + p].astype(BF)
        pad = jnp.zeros((SUB - POS, width), F32)
        out_ref[t, POS * rows :] = jnp.concatenate([both[t * POS : (t + 1) * POS], pad], axis=0).astype(BF)


def gather_y_kernel(*rest):
    n = len(Y_OFFSETS)
    pieces, outs, (acc, flat, smem, sem) = rest[:n], rest[n:-4], rest[-4:]
    rows = acc.shape[1]
    blocks = (pieces[0].shape[0] - SUB) // rows
    mx = lax.axis_index("x")
    read_places([r[blocks * rows :, LANE:] for r in pieces], flat, smem, sem)
    acc[...] = jnp.zeros_like(acc)
    for i in range(n):
        for b in range(blocks):
            acc[smem[0, i * SUB + b]] += pieces[i][b * rows : (b + 1) * rows].astype(F32)
    for i in range(NX):
        to = pl.multiple_of(lax.rem(mx + i, NX) * SUB, SUB)
        outs[i][...] = acc[:, pl.ds(to, SUB), :].astype(BF)


def vmem_call(kernel, name, out_shape, args, scratch=(), after=0):
    vm = pl.BlockSpec(memory_space=pltpu.VMEM)
    anywhere = pl.BlockSpec(memory_space=pl.ANY)
    size = sum(a.size * a.dtype.itemsize for a in args)
    return pl.pallas_call(
        kernel,
        in_specs=[vm] * (len(args) - after) + [anywhere] * after,
        out_specs=jax.tree.map(lambda _: vm, out_shape),
        out_shape=out_shape,
        scratch_shapes=list(scratch),
        compiler_params=pltpu.CompilerParams(vmem_limit_bytes=32 << 20),
        cost_estimate=pl.CostEstimate(flops=size, bytes_accessed=2 * size, transcendentals=0),
        name=name,
    )(*args)


def ring_z_kernel(*refs):
    ins, outs = refs[:NX], refs[NX + 1 :]
    mz = lax.axis_index("z")
    for i in range(NZ):
        for y in range(NY):
            at = pl.ds((y * NZ + lax.rem(mz + i, NZ)) * POS, POS)
            outs[i][y] = sum(r[at].astype(F32) for r in ins).astype(BF)


def ring_y_kernel(*refs):
    ins, outs = refs[:NZ], refs[NZ:]
    my = lax.axis_index("y")
    for i in range(NY):
        at = lax.rem(my + i, NY)
        outs[i][...] = sum(r[at].astype(F32) for r in ins)


def finish_kernel(x_ref, *rest):
    y_refs, out_ref, inv = rest[:-2], rest[-2], rest[-1]
    rows = out_ref.shape[1]
    width = x_ref.shape[2]
    my = lax.axis_index("y")
    notes = sum(x_ref[s, POS * rows :].astype(F32) for s in range(TILES))
    den = 1.0 / jnp.maximum(notes[:, :LANE] + notes[:, LANE:], 1.0)
    for p in range(POS):
        turned = jnp.transpose(jnp.broadcast_to(den[p : p + 1], (LANE, LANE)))[:rows]
        inv[p] = turned
        total = x_ref[0, p * rows : (p + 1) * rows].astype(F32)
        for s in range(1, TILES):
            total += x_ref[s, p * rows : (p + 1) * rows].astype(F32)
        for j in range(width // LANE):
            out_ref[p, :, j * LANE : (j + 1) * LANE] = total[:, j * LANE : (j + 1) * LANE] * turned
    for i in range(NY):
        at = pl.ds(pl.multiple_of(lax.rem(my - i + NY, NY) * SUB, SUB), SUB)
        for p in range(POS):
            scale = inv[p, at, :]
            for j in range(width // LANE):
                lanes = slice(width + j * LANE, width + (j + 1) * LANE)
                out_ref[p, at, lanes] = y_refs[i][p, :, j * LANE : (j + 1) * LANE] * scale


def ring(pieces, axis, size):
    out = [pieces[0]]
    for i in range(1, size):
        out.append(lax.ppermute(pieces[i], axis, [(s, (s + i) % size) for s in range(size)]))
    return out


def per_device(image, inv_var, kernel_index, dest, position, row_taps, col_taps):
    _, side, _ = image.shape
    rows, width = side // VISITS, side // 2
    shape = jax.ShapeDtypeStruct
    x_part, y_parts = match(kernel_index, dest[:, 0], position, row_taps, col_taps, image, inv_var)

    arrived = [y_parts[0]]
    for i in range(1, len(Y_OFFSETS)):
        dc, dy = Y_OFFSETS[i]
        perm = [
            (c * NY + y, ((c + dc) % NC) * NY + (y + dy) % NY) for c in range(NC) for y in range(NY)
        ]
        arrived.append(lax.ppermute(y_parts[i], ("core", "y"), perm))
    x_in = lax.all_to_all(x_part, ("x", "core"), 0, 0, tiled=True)

    scratch = [
        pltpu.VMEM((COUNT, rows, width), F32),
        pltpu.VMEM((1, LANE), jnp.int32),
        pltpu.SMEM((1, LANE), jnp.int32),
        pltpu.SemaphoreType.DMA,
    ]
    mine = vmem_call(gather_y_kernel, "gather_y", [shape((COUNT, SUB, width), BF)] * NX, arrived, scratch)
    along_x = ring(mine, "x", NX)
    x_sum = vmem_call(
        gather_x_kernel, "gather_x", shape((TILES, POS * rows + SUB, width), BF), (x_in, mine[0]), scratch, 1
    )
    x_out = lax.all_to_all(x_sum, ("y", "z"), 0, 0, tiled=True)
    along_z = vmem_call(
        ring_z_kernel, "ring_z", [shape((NY, POS, SUB, width), BF)] * NZ, (*along_x, x_sum), after=1
    )
    along_z = ring(along_z, "z", NZ)
    along_y = vmem_call(ring_y_kernel, "ring_y", [shape((POS, SUB, width), F32)] * NY, along_z)
    along_y = ring(along_y, "y", NY)
    out = vmem_call(
        finish_kernel,
        "finish",
        shape((POS, rows, side), F32),
        (x_out, *along_y),
        [pltpu.VMEM((POS, rows, LANE), F32)],
    )
    return out[None]


def solution(mesh):
    mesh = Mesh(mesh.devices.reshape(NX, NC, NY, NZ), ("x", "core", "y", "z"))
    every = ("x", "core", "y", "z")
    in_specs = (P(every, None, None), P(every, None), P(every), P(every, None), P(every), P(), P())
    out_specs = P(("y", "z"), None, ("x", "core"), None)
    return jax.shard_map(
        per_device, mesh=mesh, in_specs=in_specs, out_specs=out_specs, check_vma=False
    )
```

```python
import functools

import jax
import jax.numpy as jnp
import numpy as np
from jax import lax
from jax.experimental import pallas as pl
from jax.experimental.pallas import tpu as pltpu
from jax.sharding import Mesh, PartitionSpec as P

NB = 8
POS = 4
LANE = 128
BF = jnp.bfloat16
F32 = jnp.float32
NX, NC, NY, NZ = 4, 2, 4, 4
VISITS, TILES = NX * NC, NY * NZ
COUNT = TILES * POS
SUB = 16
VMEM_BIG = 60 << 20
WORK = 40_000_000_000
GX, GY, RZ = 40000000000, 40000000000, 1000000000
Y_OFFSETS = ((0, 0), (1, 0), (0, 1), (0, 2), (1, 2), (0, 3), (1, 1), (1, 3))


GROUP = 4


def toeplitz(row, length):
    wide = jnp.broadcast_to(row, (LANE, length))
    return pltpu.roll(wide, 0, 1, stride=1, stride_axis=0)


def band_blocks(table, taps_ref, turned):
    count = taps_ref.shape[1]
    half = (count - 1) // 2
    length = 3 * LANE
    q = lax.broadcasted_iota(jnp.int32, (count, length), 0)
    n = lax.broadcasted_iota(jnp.int32, (count, length), 1)
    hit = n - q == LANE - half if turned else n + q == LANE + half
    base = jnp.dot(taps_ref[...].astype(BF), hit.astype(F32).astype(BF), preferred_element_type=F32)
    for k in range(NB):
        table[k] = toeplitz(base[k : k + 1], length).astype(BF)


def put_band(band, block, row0, col0):
    for a in range(band.shape[0] // LANE):
        at = row0 + a
        lo, hi = max(at - 1, col0), min(at + 2, col0 + band.shape[1] // LANE)
        if lo < hi:
            off = (lo - (at - 1)) * LANE
            band[a * LANE : (a + 1) * LANE, (lo - col0) * LANE : (hi - col0) * LANE] = block[
                :, off : off + (hi - lo) * LANE
            ]


def combo_rows(dest_ref, pos_ref, blocks):
    row = lax.broadcasted_iota(jnp.int32, (SUB, LANE), 0)
    places = jnp.full((SUB, LANE), COUNT, jnp.int32)
    for b in range(blocks):
        places = jnp.where(row == b, dest_ref[b] * POS + pos_ref[b], places)
    return places.astype(F32).astype(BF)


def lane_weights(ivt, b, width):
    onehot = (lax.broadcasted_iota(jnp.int32, (LANE, LANE), 0) == b).astype(F32).astype(BF)
    weight = jnp.dot(ivt[...], onehot, preferred_element_type=F32)
    return jnp.concatenate([weight] * (width // LANE), axis=1)


def padded_weights(iv_ref):
    blocks, side = iv_ref.shape
    return jnp.concatenate([iv_ref[...].astype(F32), jnp.zeros((LANE - blocks, side), F32)], axis=0)


def match_x_kernel(kidx_ref, dest_ref, pos_ref, rtap_ref, ctap_ref, iv_ref, img_ref, x_ref, mid_ref, *scratch):
    rtab, ctab, rband, cband, ivt, image, mids, x_buf, in_sem, mid_sem, x_sem = scratch
    blocks, side = iv_ref.shape
    rows, width = side // VISITS, side // 2
    top = blocks * rows
    loads = [pltpu.make_async_copy(img_ref.at[b], image.at[b], in_sem.at[b]) for b in range(blocks)]
    for load in loads:
        load.start()

    places = combo_rows(dest_ref, pos_ref, blocks)
    weights = padded_weights(iv_ref)
    ivt[...] = jnp.transpose(weights).astype(BF)
    for v in range(VISITS):
        part = weights[:SUB, (v // 2) * LANE : (v // 2 + 1) * LANE]
        if v % 2:
            part = pltpu.roll(part, rows, 1)
        x_buf[v, top:, :LANE] = part.astype(BF)
        x_buf[v, top:, LANE:] = places
    band_blocks(rtab, rtap_ref, False)
    band_blocks(ctab, ctap_ref, True)
    rband[...] = jnp.zeros_like(rband)
    cband[...] = jnp.zeros_like(cband)

    stores = []
    for b in range(blocks):
        k = kidx_ref[b]
        put_band(rband, rtab.at[k], 0, 0)
        put_band(cband, ctab.at[k], 0, 0)
        weight = lane_weights(ivt, b, width)
        loads[b].wait()
        mid = jnp.dot(rband[...], image[b], preferred_element_type=F32).astype(BF)
        mids[b] = mid[:, LANE:]
        stores.append(pltpu.make_async_copy(mids.at[b], mid_ref.at[b], mid_sem.at[b]))
        stores[-1].start()
        matched = jnp.dot(mid[:, : 3 * LANE], cband[...], preferred_element_type=F32)
        weighted = (matched * weight).astype(BF)
        for v in range(VISITS):
            x_buf[v, b * rows : (b + 1) * rows] = weighted[v * rows : (v + 1) * rows]
        if (b + 1) % GROUP == 0 or b + 1 == blocks:
            g = b // GROUP
            first = g * GROUP * rows
            last = (b + 1) * rows + (SUB if b + 1 == blocks else 0)
            part = pl.ds(first, last - first)
            stores.append(pltpu.make_async_copy(x_buf.at[:, part], x_ref.at[:, part], x_sem.at[g]))
            stores[-1].start()
    for store in stores:
        store.wait()


def match_y_kernel(kidx_ref, dest_ref, pos_ref, ctap_ref, iv_ref, mid_ref, *rest):
    n = len(Y_OFFSETS)
    y_refs = rest[:n]
    ctab, cband, ivt, mids, y_buf, whole, in_sem, y_sem = rest[n:]
    blocks, side = iv_ref.shape
    tiles, rows, width = side // LANE, side // VISITS, side // 2
    top = blocks * rows
    loads = [pltpu.make_async_copy(mid_ref.at[b], mids.at[b], in_sem.at[b]) for b in range(blocks)]
    for load in loads:
        load.start()

    places = combo_rows(dest_ref, pos_ref, blocks)
    ivt[...] = jnp.transpose(padded_weights(iv_ref)).astype(BF)
    for i in range(n):
        y_buf[i, top:, :LANE] = places
        y_buf[i, top:, LANE:] = places
    band_blocks(ctab, ctap_ref, True)
    cband[...] = jnp.zeros_like(cband)

    mc, my = lax.axis_index("core"), lax.axis_index("y")
    stores = []
    for b in range(blocks):
        put_band(cband, ctab.at[kidx_ref[b]], tiles - 3, tiles // 2)
        weight = lane_weights(ivt, b, width)
        loads[b].wait()
        matched = jnp.dot(mids[b], cband[...], preferred_element_type=F32)
        whole[b % 2] = (matched * weight).astype(BF)
        for i, (dc, dy) in enumerate(Y_OFFSETS):
            core, sub = lax.rem(mc + dc, NC), lax.rem(my + dy, NY)
            for x in range(NX):
                start = pl.multiple_of((x * NC + core) * rows + sub * SUB, SUB)
                y_buf[i, b * rows + x * SUB : b * rows + (x + 1) * SUB] = whole[b % 2, pl.ds(start, SUB), :]
        if (b + 1) % GROUP == 0 or b + 1 == blocks:
            g = b // GROUP
            first = g * GROUP * rows
            last = (b + 1) * rows + (SUB if b + 1 == blocks else 0)
            part = pl.ds(first, last - first)
            for i in range(n):
                stores.append(pltpu.make_async_copy(y_buf.at[i, part], y_refs[i].at[part], y_sem.at[g, i]))
                stores[-1].start()
    for store in stores:
        store.wait()


def match(kidx, dest, position, row_taps, col_taps, image, inv_var):
    blocks, side, _ = image.shape
    rows, width = side // VISITS, side // 2
    tall = blocks * rows + SUB
    groups = -(-blocks // GROUP)
    n = len(Y_OFFSETS)
    smem = pl.BlockSpec(memory_space=pltpu.SMEM)
    vmem = pl.BlockSpec(memory_space=pltpu.VMEM)
    hbm = pl.BlockSpec(memory_space=pltpu.HBM)
    table = pltpu.VMEM((NB, LANE, 3 * LANE), BF)
    band = pltpu.VMEM((3 * LANE, width), BF)
    turned = pltpu.VMEM((side, LANE), BF)
    sems = pltpu.SemaphoreType.DMA
    shape = jax.ShapeDtypeStruct
    rest = (blocks, side, side - LANE)
    params = pltpu.CompilerParams(vmem_limit_bytes=VMEM_BIG)
    cost = pl.CostEstimate(flops=WORK, bytes_accessed=image.size * 4, transcendentals=0)
    x_part, mid = pl.pallas_call(
        match_x_kernel,
        in_specs=[smem] * 3 + [vmem] * 3 + [hbm],
        out_specs=[hbm] * 2,
        out_shape=[shape((VISITS, tall, width), BF), shape(rest, BF)],
        scratch_shapes=[
            table,
            table,
            pltpu.VMEM((side, side), BF),
            band,
            turned,
            pltpu.VMEM(image.shape, BF),
            pltpu.VMEM(rest, BF),
            pltpu.VMEM((VISITS, tall, width), BF),
            sems((blocks,)),
            sems((blocks,)),
            sems((groups,)),
        ],
        compiler_params=params,
        cost_estimate=cost,
        name="match_x",
    )(kidx, dest, position, row_taps, col_taps, inv_var, image)
    y_parts = pl.pallas_call(
        match_y_kernel,
        in_specs=[smem] * 3 + [vmem] * 2 + [hbm],
        out_specs=[hbm] * n,
        out_shape=[shape((tall, width), BF)] * n,
        scratch_shapes=[
            table,
            band,
            turned,
            pltpu.VMEM(rest, BF),
            pltpu.VMEM((n, tall, width), BF),
            pltpu.VMEM((2, side, width), BF),
            sems((blocks,)),
            sems((groups, n)),
        ],
        compiler_params=params,
        cost_estimate=cost,
        name="match_y",
    )(kidx, dest, position, col_taps, inv_var, mid)
    return x_part, y_parts


def read_places(notes, flat, smem, sem):
    places = jnp.concatenate([n.astype(F32) for n in notes], axis=0)
    size = VISITS * SUB
    row = lax.broadcasted_iota(jnp.int32, (size, LANE), 0)
    lane = lax.broadcasted_iota(jnp.int32, (size, LANE), 1)
    line = jnp.sum(jnp.where(row == lane, places, 0.0), axis=0, keepdims=True)
    flat[...] = line.astype(jnp.int32)
    copy = pltpu.make_async_copy(flat, smem, sem)
    copy.start()
    copy.wait()
    return line


def gather_x_kernel(in_ref, out_hbm, acc, flat, smem, sem, out_ref, out_sem):
    rows, width = acc.shape[1:]
    blocks = (in_ref.shape[1] - SUB) // rows
    top = blocks * rows
    line = read_places([in_ref[v, top:, LANE:] for v in range(VISITS)], flat, smem, sem)
    acc[...] = jnp.zeros_like(acc)
    for v in range(VISITS):
        for b in range(blocks):
            acc[smem[0, v * SUB + b]] += in_ref[v, b * rows : (b + 1) * rows].astype(F32)
    place = lax.broadcasted_iota(jnp.int32, (COUNT, LANE), 0)
    hit = (place == line.astype(jnp.int32)).astype(F32).astype(BF)
    weights = jnp.concatenate([in_ref[v, top:, :LANE].astype(F32) for v in range(VISITS)], axis=0).astype(BF)
    den = jnp.dot(hit, weights, preferred_element_type=F32)
    high = den.astype(BF).astype(F32)
    both = jnp.concatenate([high, den - high], axis=1)
    stores = []
    for t in range(TILES):
        for p in range(POS):
            out_ref[t, p * rows : (p + 1) * rows] = acc[t * POS + p].astype(BF)
        pad = jnp.zeros((SUB - POS, width), F32)
        out_ref[t, POS * rows :] = jnp.concatenate([both[t * POS : (t + 1) * POS], pad], axis=0).astype(BF)
        if (t + 1) % GROUP == 0:
            part = pl.ds(t + 1 - GROUP, GROUP)
            stores.append(pltpu.make_async_copy(out_ref.at[part], out_hbm.at[part], out_sem.at[t // GROUP]))
            stores[-1].start()
    for store in stores:
        store.wait()


def gather_y_kernel(*rest):
    n = len(Y_OFFSETS)
    pieces, outs, (acc, flat, smem, sem, out_buf, out_sem) = rest[:n], rest[n + 1 : -6], rest[-6:]
    rows = acc.shape[1]
    blocks = (pieces[0].shape[0] - SUB) // rows
    mx = lax.axis_index("x")
    read_places([r[blocks * rows :, LANE:] for r in pieces], flat, smem, sem)
    acc[...] = jnp.zeros_like(acc)
    for i in range(n):
        for b in range(blocks):
            acc[smem[0, i * SUB + b]] += pieces[i][b * rows : (b + 1) * rows].astype(F32)
    stores = [pltpu.make_async_copy(out_buf.at[i], outs[i], out_sem.at[i]) for i in range(NX)]
    for i in range(NX):
        to = pl.multiple_of(lax.rem(mx + i, NX) * SUB, SUB)
        out_buf[i] = acc[:, pl.ds(to, SUB), :].astype(BF)
        stores[i].start()
    for store in stores:
        store.wait()


def vmem_call(kernel, name, out_shape, args, scratch=(), after=0, flops=0, hbm_out=False):
    vm = pl.BlockSpec(memory_space=pltpu.VMEM)
    anywhere = pl.BlockSpec(memory_space=pl.ANY)
    size = sum(a.size * a.dtype.itemsize for a in args)
    flops = flops or size
    return pl.pallas_call(
        kernel,
        in_specs=[vm] * (len(args) - after) + [anywhere] * after,
        out_specs=jax.tree.map(lambda _: pl.BlockSpec(memory_space=pltpu.HBM) if hbm_out else vm, out_shape),
        out_shape=out_shape,
        scratch_shapes=list(scratch),
        compiler_params=pltpu.CompilerParams(vmem_limit_bytes=32 << 20),
        cost_estimate=pl.CostEstimate(flops=flops, bytes_accessed=2 * size, transcendentals=0),
        name=name,
    )(*args)


def ring_z_kernel(*refs):
    ins, outs = refs[:NX], refs[NX:]
    mz = lax.axis_index("z")
    for i in range(NZ):
        for y in range(NY):
            at = pl.ds((y * NZ + lax.rem(mz + i, NZ)) * POS, POS)
            outs[i][y] = sum(r[at].astype(F32) for r in ins).astype(BF)


def ring_y_kernel(*refs):
    ins, outs = refs[:NZ], refs[NZ:]
    my = lax.axis_index("y")
    for i in range(NY):
        at = lax.rem(my + i, NY)
        outs[i][...] = sum(r[at].astype(F32) for r in ins)


def finish_kernel(x_ref, *rest):
    y_refs, out_ref, inv = rest[:-2], rest[-2], rest[-1]
    rows = out_ref.shape[1]
    width = x_ref.shape[2]
    my = lax.axis_index("y")
    notes = sum(x_ref[s, POS * rows :].astype(F32) for s in range(TILES))
    den = 1.0 / jnp.maximum(notes[:, :LANE] + notes[:, LANE:], 1.0)
    for p in range(POS):
        turned = jnp.transpose(jnp.broadcast_to(den[p : p + 1], (LANE, LANE)))[:rows]
        inv[p] = turned
        total = x_ref[0, p * rows : (p + 1) * rows].astype(F32)
        for s in range(1, TILES):
            total += x_ref[s, p * rows : (p + 1) * rows].astype(F32)
        for j in range(width // LANE):
            out_ref[p, :, j * LANE : (j + 1) * LANE] = total[:, j * LANE : (j + 1) * LANE] * turned
    for i in range(NY):
        at = pl.ds(pl.multiple_of(lax.rem(my - i + NY, NY) * SUB, SUB), SUB)
        for p in range(POS):
            scale = inv[p, at, :]
            for j in range(width // LANE):
                lanes = slice(width + j * LANE, width + (j + 1) * LANE)
                out_ref[p, at, lanes] = y_refs[i][p, :, j * LANE : (j + 1) * LANE] * scale


def ring(pieces, axis, size):
    out = [pieces[0]]
    for i in range(1, size):
        out.append(lax.ppermute(pieces[i], axis, [(s, (s + i) % size) for s in range(size)]))
    return out


def per_device(image, inv_var, kernel_index, dest, position, row_taps, col_taps):
    _, side, _ = image.shape
    rows, width = side // VISITS, side // 2
    shape = jax.ShapeDtypeStruct
    x_part, y_parts = match(kernel_index, dest[:, 0], position, row_taps, col_taps, image, inv_var)

    arrived = [y_parts[0]]
    for i in range(1, len(Y_OFFSETS)):
        dc, dy = Y_OFFSETS[i]
        perm = [
            (c * NY + y, ((c + dc) % NC) * NY + (y + dy) % NY) for c in range(NC) for y in range(NY)
        ]
        arrived.append(lax.ppermute(y_parts[i], ("core", "y"), perm))
    x_in = lax.all_to_all(x_part, ("x", "core"), 0, 0, tiled=True)

    scratch = [
        pltpu.VMEM((COUNT, rows, width), F32),
        pltpu.VMEM((1, LANE), jnp.int32),
        pltpu.SMEM((1, LANE), jnp.int32),
        pltpu.SemaphoreType.DMA,
    ]
    y_scratch = scratch + [pltpu.VMEM((NX, COUNT, SUB, width), BF), pltpu.SemaphoreType.DMA((NX,))]
    x_scratch = scratch + [
        pltpu.VMEM((TILES, POS * rows + SUB, width), BF),
        pltpu.SemaphoreType.DMA((TILES // GROUP,)),
    ]
    x_sum = vmem_call(
        gather_x_kernel, "gather_x", shape((TILES, POS * rows + SUB, width), BF), (x_in,), x_scratch, 0, GX, True
    )
    mine = vmem_call(gather_y_kernel, "gather_y", [shape((COUNT, SUB, width), BF)] * NX, (*arrived, x_sum), y_scratch, 1, GY, True)
    along_x = ring(mine, "x", NX)
    x_out = lax.all_to_all(x_sum, ("y", "z"), 0, 0, tiled=True)
    along_z = vmem_call(
        ring_z_kernel, "ring_z", [shape((NY, POS, SUB, width), BF)] * NZ, along_x, flops=RZ
    )
    along_z = ring(along_z, "z", NZ)
    along_y = vmem_call(ring_y_kernel, "ring_y", [shape((POS, SUB, width), F32)] * NY, along_z)
    along_y = ring(along_y, "y", NY)
    out = vmem_call(
        finish_kernel,
        "finish",
        shape((POS, rows, side), F32),
        (x_out, *along_y),
        [pltpu.VMEM((POS, rows, LANE), F32)],
    )
    return out[None]


def solution(mesh):
    mesh = Mesh(mesh.devices.reshape(NX, NC, NY, NZ), ("x", "core", "y", "z"))
    every = ("x", "core", "y", "z")
    in_specs = (P(every, None, None), P(every, None), P(every), P(every, None), P(every), P(), P())
    out_specs = P(("y", "z"), None, ("x", "core"), None)
    return jax.shard_map(
        per_device, mesh=mesh, in_specs=in_specs, out_specs=out_specs, check_vma=False
    )
```

```python
import functools

import jax
import jax.numpy as jnp
import numpy as np
from jax import lax
from jax.experimental import pallas as pl
from jax.experimental.pallas import tpu as pltpu
from jax.sharding import Mesh, PartitionSpec as P

NB = 8
POS = 4
LANE = 128
BF = jnp.bfloat16
F32 = jnp.float32
NX, NC, NY, NZ = 4, 2, 4, 4
VISITS, TILES = NX * NC, NY * NZ
COUNT = TILES * POS
SUB = 16
VMEM_BIG = 60 << 20
WORK = 40_000_000_000
GX, GY, RZ = 40000000000, 40000000000, 1000000000
Y_OFFSETS = ((0, 0), (1, 0), (0, 1), (0, 2), (1, 2), (0, 3), (1, 1), (1, 3))


GROUP = 4
RING_ORDER = (2, 1, 3)
AHEAD = 3


def toeplitz(row, length):
    wide = jnp.broadcast_to(row, (LANE, length))
    return pltpu.roll(wide, 0, 1, stride=1, stride_axis=0)


def band_blocks(table, taps_ref, turned):
    count = taps_ref.shape[1]
    half = (count - 1) // 2
    length = 3 * LANE
    q = lax.broadcasted_iota(jnp.int32, (count, length), 0)
    n = lax.broadcasted_iota(jnp.int32, (count, length), 1)
    hit = n - q == LANE - half if turned else n + q == LANE + half
    base = jnp.dot(taps_ref[...].astype(BF), hit.astype(F32).astype(BF), preferred_element_type=F32)
    for k in range(NB):
        table[k] = toeplitz(base[k : k + 1], length).astype(BF)


def put_band(band, block, row0, col0):
    for a in range(band.shape[0] // LANE):
        at = row0 + a
        lo, hi = max(at - 1, col0), min(at + 2, col0 + band.shape[1] // LANE)
        if lo < hi:
            off = (lo - (at - 1)) * LANE
            band[a * LANE : (a + 1) * LANE, (lo - col0) * LANE : (hi - col0) * LANE] = block[
                :, off : off + (hi - lo) * LANE
            ]


def combo_rows(dest_ref, pos_ref, blocks):
    row = lax.broadcasted_iota(jnp.int32, (SUB, LANE), 0)
    places = jnp.full((SUB, LANE), COUNT, jnp.int32)
    for b in range(blocks):
        places = jnp.where(row == b, dest_ref[b] * POS + pos_ref[b], places)
    return places.astype(F32).astype(BF)


def lane_weights(ivt, b, width):
    onehot = (lax.broadcasted_iota(jnp.int32, (LANE, LANE), 0) == b).astype(F32).astype(BF)
    weight = jnp.dot(ivt[...], onehot, preferred_element_type=F32)
    return jnp.concatenate([weight] * (width // LANE), axis=1)


def padded_weights(iv_ref):
    blocks, side = iv_ref.shape
    return jnp.concatenate([iv_ref[...].astype(F32), jnp.zeros((LANE - blocks, side), F32)], axis=0)


def match_x_kernel(kidx_ref, dest_ref, pos_ref, rtap_ref, ctap_ref, iv_ref, img_ref, x_ref, mid_ref, *scratch):
    rtab, ctab, rband, cband, ivt, image, mids, x_buf, in_sem, mid_sem, x_sem = scratch
    blocks, side = iv_ref.shape
    rows, width = side // VISITS, side // 2
    top = blocks * rows
    loads = [pltpu.make_async_copy(img_ref.at[b], image.at[b], in_sem.at[b]) for b in range(blocks)]
    for load in loads[:AHEAD]:
        load.start()

    places = combo_rows(dest_ref, pos_ref, blocks)
    weights = padded_weights(iv_ref)
    ivt[...] = jnp.transpose(weights).astype(BF)
    for v in range(VISITS):
        part = weights[:SUB, (v // 2) * LANE : (v // 2 + 1) * LANE]
        if v % 2:
            part = pltpu.roll(part, rows, 1)
        x_buf[v, top:, :LANE] = part.astype(BF)
        x_buf[v, top:, LANE:] = places
    band_blocks(rtab, rtap_ref, False)
    band_blocks(ctab, ctap_ref, True)
    rband[...] = jnp.zeros_like(rband)
    cband[...] = jnp.zeros_like(cband)

    stores = []
    for b in range(blocks):
        k = kidx_ref[b]
        put_band(rband, rtab.at[k], 0, 0)
        put_band(cband, ctab.at[k], 0, 0)
        weight = lane_weights(ivt, b, width)
        loads[b].wait()
        if b + AHEAD < blocks:
            loads[b + AHEAD].start()
        mid = jnp.dot(rband[...], image[b], preferred_element_type=F32).astype(BF)
        mids[b] = mid[:, LANE:]
        stores.append(pltpu.make_async_copy(mids.at[b], mid_ref.at[b], mid_sem.at[b]))
        stores[-1].start()
        matched = jnp.dot(mid[:, : 3 * LANE], cband[...], preferred_element_type=F32)
        weighted = (matched * weight).astype(BF)
        for v in range(VISITS):
            x_buf[v, b * rows : (b + 1) * rows] = weighted[v * rows : (v + 1) * rows]
        if (b + 1) % GROUP == 0 or b + 1 == blocks:
            g = b // GROUP
            first = g * GROUP * rows
            last = (b + 1) * rows + (SUB if b + 1 == blocks else 0)
            part = pl.ds(first, last - first)
            stores.append(pltpu.make_async_copy(x_buf.at[:, part], x_ref.at[:, part], x_sem.at[g]))
            stores[-1].start()
    for store in stores:
        store.wait()


def match_y_kernel(kidx_ref, dest_ref, pos_ref, ctap_ref, iv_ref, mid_ref, *rest):
    n = len(Y_OFFSETS)
    y_refs = rest[:n]
    ctab, cband, ivt, mids, y_buf, whole, in_sem, y_sem = rest[n:]
    blocks, side = iv_ref.shape
    tiles, rows, width = side // LANE, side // VISITS, side // 2
    top = blocks * rows
    loads = [pltpu.make_async_copy(mid_ref.at[b], mids.at[b], in_sem.at[b]) for b in range(blocks)]
    for load in loads[:AHEAD]:
        load.start()

    places = combo_rows(dest_ref, pos_ref, blocks)
    ivt[...] = jnp.transpose(padded_weights(iv_ref)).astype(BF)
    for i in range(n):
        y_buf[i, top:, :LANE] = places
        y_buf[i, top:, LANE:] = places
    band_blocks(ctab, ctap_ref, True)
    cband[...] = jnp.zeros_like(cband)

    mc, my = lax.axis_index("core"), lax.axis_index("y")
    stores = []
    for b in range(blocks):
        put_band(cband, ctab.at[kidx_ref[b]], tiles - 3, tiles // 2)
        weight = lane_weights(ivt, b, width)
        loads[b].wait()
        if b + AHEAD < blocks:
            loads[b + AHEAD].start()
        matched = jnp.dot(mids[b], cband[...], preferred_element_type=F32)
        whole[b % 2] = (matched * weight).astype(BF)
        for i, (dc, dy) in enumerate(Y_OFFSETS):
            core, sub = lax.rem(mc + dc, NC), lax.rem(my + dy, NY)
            for x in range(NX):
                start = pl.multiple_of((x * NC + core) * rows + sub * SUB, SUB)
                y_buf[i, b * rows + x * SUB : b * rows + (x + 1) * SUB] = whole[b % 2, pl.ds(start, SUB), :]
        if (b + 1) % GROUP == 0 or b + 1 == blocks:
            g = b // GROUP
            first = g * GROUP * rows
            last = (b + 1) * rows + (SUB if b + 1 == blocks else 0)
            part = pl.ds(first, last - first)
            for i in range(n):
                stores.append(pltpu.make_async_copy(y_buf.at[i, part], y_refs[i].at[part], y_sem.at[g, i]))
                stores[-1].start()
    for store in stores:
        store.wait()


def match(kidx, dest, position, row_taps, col_taps, image, inv_var):
    blocks, side, _ = image.shape
    rows, width = side // VISITS, side // 2
    tall = blocks * rows + SUB
    groups = -(-blocks // GROUP)
    n = len(Y_OFFSETS)
    smem = pl.BlockSpec(memory_space=pltpu.SMEM)
    vmem = pl.BlockSpec(memory_space=pltpu.VMEM)
    hbm = pl.BlockSpec(memory_space=pltpu.HBM)
    table = pltpu.VMEM((NB, LANE, 3 * LANE), BF)
    band = pltpu.VMEM((3 * LANE, width), BF)
    turned = pltpu.VMEM((side, LANE), BF)
    sems = pltpu.SemaphoreType.DMA
    shape = jax.ShapeDtypeStruct
    rest = (blocks, side, side - LANE)
    params = pltpu.CompilerParams(vmem_limit_bytes=VMEM_BIG)
    cost = pl.CostEstimate(flops=WORK, bytes_accessed=image.size * 4, transcendentals=0)
    x_part, mid = pl.pallas_call(
        match_x_kernel,
        in_specs=[smem] * 3 + [vmem] * 3 + [hbm],
        out_specs=[hbm] * 2,
        out_shape=[shape((VISITS, tall, width), BF), shape(rest, BF)],
        scratch_shapes=[
            table,
            table,
            pltpu.VMEM((side, side), BF),
            band,
            turned,
            pltpu.VMEM(image.shape, BF),
            pltpu.VMEM(rest, BF),
            pltpu.VMEM((VISITS, tall, width), BF),
            sems((blocks,)),
            sems((blocks,)),
            sems((groups,)),
        ],
        compiler_params=params,
        cost_estimate=cost,
        name="match_x",
    )(kidx, dest, position, row_taps, col_taps, inv_var, image)
    y_parts = pl.pallas_call(
        match_y_kernel,
        in_specs=[smem] * 3 + [vmem] * 2 + [hbm],
        out_specs=[hbm] * n,
        out_shape=[shape((tall, width), BF)] * n,
        scratch_shapes=[
            table,
            band,
            turned,
            pltpu.VMEM(rest, BF),
            pltpu.VMEM((n, tall, width), BF),
            pltpu.VMEM((2, side, width), BF),
            sems((blocks,)),
            sems((groups, n)),
        ],
        compiler_params=params,
        cost_estimate=cost,
        name="match_y",
    )(kidx, dest, position, col_taps, inv_var, mid)
    return x_part, y_parts


def read_places(notes, flat, smem, sem):
    places = jnp.concatenate([n.astype(F32) for n in notes], axis=0)
    size = VISITS * SUB
    row = lax.broadcasted_iota(jnp.int32, (size, LANE), 0)
    lane = lax.broadcasted_iota(jnp.int32, (size, LANE), 1)
    line = jnp.sum(jnp.where(row == lane, places, 0.0), axis=0, keepdims=True)
    flat[...] = line.astype(jnp.int32)
    copy = pltpu.make_async_copy(flat, smem, sem)
    copy.start()
    copy.wait()
    return line


def gather_x_kernel(in_ref, out_hbm, done_ref, acc, flat, smem, sem, out_ref, out_sem):
    rows, width = acc.shape[1:]
    blocks = (in_ref.shape[1] - SUB) // rows
    top = blocks * rows
    done_ref[...] = jnp.zeros_like(done_ref)
    line = read_places([in_ref[v, top:, LANE:] for v in range(VISITS)], flat, smem, sem)
    acc[...] = jnp.zeros_like(acc)
    for v in range(VISITS):
        for b in range(blocks):
            acc[smem[0, v * SUB + b]] += in_ref[v, b * rows : (b + 1) * rows].astype(F32)
    place = lax.broadcasted_iota(jnp.int32, (COUNT, LANE), 0)
    hit = (place == line.astype(jnp.int32)).astype(F32).astype(BF)
    weights = jnp.concatenate([in_ref[v, top:, :LANE].astype(F32) for v in range(VISITS)], axis=0).astype(BF)
    den = jnp.dot(hit, weights, preferred_element_type=F32)
    high = den.astype(BF).astype(F32)
    both = jnp.concatenate([high, den - high], axis=1)
    stores = []
    for t in range(TILES):
        for p in range(POS):
            out_ref[t, p * rows : (p + 1) * rows] = acc[t * POS + p].astype(BF)
        pad = jnp.zeros((SUB - POS, width), F32)
        out_ref[t, POS * rows :] = jnp.concatenate([both[t * POS : (t + 1) * POS], pad], axis=0).astype(BF)
        if (t + 1) % GROUP == 0:
            part = pl.ds(t + 1 - GROUP, GROUP)
            stores.append(pltpu.make_async_copy(out_ref.at[part], out_hbm.at[part], out_sem.at[t // GROUP]))
            stores[-1].start()
    for store in stores:
        store.wait()


def gather_y_kernel(*rest):
    n = len(Y_OFFSETS)
    pieces, outs, (acc, flat, smem, sem, out_buf, out_sem) = rest[:n], rest[n + 1 : -6], rest[-6:]
    rows = acc.shape[1]
    blocks = (pieces[0].shape[0] - SUB) // rows
    mx = lax.axis_index("x")
    read_places([r[blocks * rows :, LANE:] for r in pieces], flat, smem, sem)
    acc[...] = jnp.zeros_like(acc)
    for i in range(n):
        for b in range(blocks):
            acc[smem[0, i * SUB + b]] += pieces[i][b * rows : (b + 1) * rows].astype(F32)
    stores = [pltpu.make_async_copy(out_buf.at[i], outs[i], out_sem.at[i]) for i in range(NX)]
    for i in range(NX):
        to = pl.multiple_of(lax.rem(mx + i, NX) * SUB, SUB)
        out_buf[i] = acc[:, pl.ds(to, SUB), :].astype(BF)
        stores[i].start()
    for store in stores:
        store.wait()


def vmem_call(kernel, name, out_shape, args, scratch=(), after=0, flops=0, hbm_out=False):
    hbm_out = hbm_out or jax.tree.map(lambda _: False, out_shape)
    vm = pl.BlockSpec(memory_space=pltpu.VMEM)
    anywhere = pl.BlockSpec(memory_space=pl.ANY)
    size = sum(a.size * a.dtype.itemsize for a in args)
    flops = flops or size
    return pl.pallas_call(
        kernel,
        in_specs=[vm] * (len(args) - after) + [anywhere] * after,
        out_specs=jax.tree.map(lambda far: pl.BlockSpec(memory_space=pltpu.HBM) if far else vm, hbm_out),
        out_shape=out_shape,
        scratch_shapes=list(scratch),
        compiler_params=pltpu.CompilerParams(vmem_limit_bytes=32 << 20),
        cost_estimate=pl.CostEstimate(flops=flops, bytes_accessed=2 * size, transcendentals=0),
        name=name,
    )(*args)


def ring_z_kernel(*refs):
    ins, outs = refs[:NX], refs[NX:]
    mz = lax.axis_index("z")
    for i in range(NZ):
        for y in range(NY):
            at = pl.ds((y * NZ + lax.rem(mz + i, NZ)) * POS, POS)
            outs[i][y] = sum(r[at].astype(F32) for r in ins).astype(BF)


def ring_y_kernel(*refs):
    ins, outs = refs[:NZ], refs[NZ:]
    my = lax.axis_index("y")
    for i in range(NY):
        at = lax.rem(my + i, NY)
        outs[i][...] = sum(r[at].astype(F32) for r in ins)


def finish_kernel(x_ref, *rest):
    y_refs, out_ref, inv = rest[:-2], rest[-2], rest[-1]
    rows = out_ref.shape[1]
    width = x_ref.shape[2]
    my = lax.axis_index("y")
    notes = sum(x_ref[s, POS * rows :].astype(F32) for s in range(TILES))
    den = 1.0 / jnp.maximum(notes[:, :LANE] + notes[:, LANE:], 1.0)
    for p in range(POS):
        turned = jnp.transpose(jnp.broadcast_to(den[p : p + 1], (LANE, LANE)))[:rows]
        inv[p] = turned
        total = x_ref[0, p * rows : (p + 1) * rows].astype(F32)
        for s in range(1, TILES):
            total += x_ref[s, p * rows : (p + 1) * rows].astype(F32)
        for j in range(width // LANE):
            out_ref[p, :, j * LANE : (j + 1) * LANE] = total[:, j * LANE : (j + 1) * LANE] * turned
    for i, step in enumerate((0,) + RING_ORDER):
        at = pl.ds(pl.multiple_of(lax.rem(my - step + NY, NY) * SUB, SUB), SUB)
        for p in range(POS):
            scale = inv[p, at, :]
            for j in range(width // LANE):
                lanes = slice(width + j * LANE, width + (j + 1) * LANE)
                out_ref[p, at, lanes] = y_refs[i][p, :, j * LANE : (j + 1) * LANE] * scale


def ring(pieces, axis, size):
    out = [pieces[0]]
    for i in RING_ORDER:
        out.append(lax.ppermute(pieces[i], axis, [(s, (s + i) % size) for s in range(size)]))
    return out


def per_device(image, inv_var, kernel_index, dest, position, row_taps, col_taps):
    _, side, _ = image.shape
    rows, width = side // VISITS, side // 2
    shape = jax.ShapeDtypeStruct
    x_part, y_parts = match(kernel_index, dest[:, 0], position, row_taps, col_taps, image, inv_var)

    arrived = [y_parts[0]]
    for i in range(1, len(Y_OFFSETS)):
        dc, dy = Y_OFFSETS[i]
        perm = [
            (c * NY + y, ((c + dc) % NC) * NY + (y + dy) % NY) for c in range(NC) for y in range(NY)
        ]
        arrived.append(lax.ppermute(y_parts[i], ("core", "y"), perm))
    x_in = lax.all_to_all(x_part, ("x", "core"), 0, 0, tiled=True)

    scratch = [
        pltpu.VMEM((COUNT, rows, width), F32),
        pltpu.VMEM((1, LANE), jnp.int32),
        pltpu.SMEM((1, LANE), jnp.int32),
        pltpu.SemaphoreType.DMA,
    ]
    y_scratch = scratch + [pltpu.VMEM((NX, COUNT, SUB, width), BF), pltpu.SemaphoreType.DMA((NX,))]
    x_scratch = scratch + [
        pltpu.VMEM((TILES, POS * rows + SUB, width), BF),
        pltpu.SemaphoreType.DMA((TILES // GROUP,)),
    ]
    x_sum, x_done = vmem_call(
        gather_x_kernel, "gather_x", (shape((TILES, POS * rows + SUB, width), BF), shape((8, LANE), F32)), (x_in,), x_scratch, 0, GX, (True, False)
    )
    mine = vmem_call(gather_y_kernel, "gather_y", [shape((COUNT, SUB, width), BF)] * NX, (*arrived, x_done), y_scratch, 1, GY, [True] * NX)
    along_x = ring(mine, "x", NX)
    x_out = lax.all_to_all(x_sum, ("y", "z"), 0, 0, tiled=True)
    along_z = vmem_call(
        ring_z_kernel, "ring_z", [shape((NY, POS, SUB, width), BF)] * NZ, along_x, flops=RZ
    )
    along_z = ring(along_z, "z", NZ)
    along_y = vmem_call(ring_y_kernel, "ring_y", [shape((POS, SUB, width), F32)] * NY, along_z)
    along_y = ring(along_y, "y", NY)
    out = vmem_call(
        finish_kernel,
        "finish",
        shape((POS, rows, side), F32),
        (x_out, *along_y),
        [pltpu.VMEM((POS, rows, LANE), F32)],
    )
    return out[None]


def solution(mesh):
    mesh = Mesh(mesh.devices.reshape(NX, NC, NY, NZ), ("x", "core", "y", "z"))
    every = ("x", "core", "y", "z")
    in_specs = (P(every, None, None), P(every, None), P(every), P(every, None), P(every), P(), P())
    out_specs = P(("y", "z"), None, ("x", "core"), None)
    return jax.shard_map(
        per_device, mesh=mesh, in_specs=in_specs, out_specs=out_specs, check_vma=False
    )
```

```python
import functools

import jax
import jax.numpy as jnp
import numpy as np
from jax import lax
from jax.experimental import pallas as pl
from jax.experimental.pallas import tpu as pltpu
from jax.sharding import Mesh, PartitionSpec as P

NB = 8
POS = 4
LANE = 128
BF = jnp.bfloat16
F32 = jnp.float32
NX, NC, NY, NZ = 4, 2, 4, 4
VISITS, TILES = NX * NC, NY * NZ
COUNT = TILES * POS
SUB = 16
VMEM_BIG = 60 << 20
WORK = 40_000_000_000
GX, GY, RZ = 40000000000, 40000000000, 1000000000
Y_OFFSETS = ((0, 0), (1, 0), (0, 1), (0, 2), (1, 2), (0, 3), (1, 1), (1, 3))


GROUP = 2
RING_ORDER = (2, 1, 3)
AHEAD = 3


def toeplitz(row, length):
    wide = jnp.broadcast_to(row, (LANE, length))
    return pltpu.roll(wide, 0, 1, stride=1, stride_axis=0)


def band_blocks(table, taps_ref, turned):
    count = taps_ref.shape[1]
    half = (count - 1) // 2
    length = 3 * LANE
    q = lax.broadcasted_iota(jnp.int32, (count, length), 0)
    n = lax.broadcasted_iota(jnp.int32, (count, length), 1)
    hit = n - q == LANE - half if turned else n + q == LANE + half
    base = jnp.dot(taps_ref[...].astype(BF), hit.astype(F32).astype(BF), preferred_element_type=F32)
    for k in range(NB):
        table[k] = toeplitz(base[k : k + 1], length).astype(BF)


def put_band(band, block, row0, col0):
    for a in range(band.shape[0] // LANE):
        at = row0 + a
        lo, hi = max(at - 1, col0), min(at + 2, col0 + band.shape[1] // LANE)
        if lo < hi:
            off = (lo - (at - 1)) * LANE
            band[a * LANE : (a + 1) * LANE, (lo - col0) * LANE : (hi - col0) * LANE] = block[
                :, off : off + (hi - lo) * LANE
            ]


def combo_rows(dest_ref, pos_ref, blocks):
    row = lax.broadcasted_iota(jnp.int32, (SUB, LANE), 0)
    places = jnp.full((SUB, LANE), COUNT, jnp.int32)
    for b in range(blocks):
        places = jnp.where(row == b, dest_ref[b] * POS + pos_ref[b], places)
    return places.astype(F32).astype(BF)


def lane_weights(ivt, b, width):
    onehot = (lax.broadcasted_iota(jnp.int32, (LANE, LANE), 0) == b).astype(F32).astype(BF)
    weight = jnp.dot(ivt[...], onehot, preferred_element_type=F32)
    return jnp.concatenate([weight] * (width // LANE), axis=1)


def padded_weights(iv_ref):
    blocks, side = iv_ref.shape
    return jnp.concatenate([iv_ref[...].astype(F32), jnp.zeros((LANE - blocks, side), F32)], axis=0)


def match_x_kernel(kidx_ref, dest_ref, pos_ref, rtap_ref, ctap_ref, iv_ref, img_ref, x_ref, mid_ref, *scratch):
    rtab, ctab, rband, cband, ivt, image, mids, x_buf, in_sem, mid_sem, x_sem = scratch
    blocks, side = iv_ref.shape
    rows, width = side // VISITS, side // 2
    top = blocks * rows
    loads = [pltpu.make_async_copy(img_ref.at[b], image.at[b], in_sem.at[b]) for b in range(blocks)]
    for load in loads[:AHEAD]:
        load.start()

    places = combo_rows(dest_ref, pos_ref, blocks)
    weights = padded_weights(iv_ref)
    ivt[...] = jnp.transpose(weights).astype(BF)
    for v in range(VISITS):
        part = weights[:SUB, (v // 2) * LANE : (v // 2 + 1) * LANE]
        if v % 2:
            part = pltpu.roll(part, rows, 1)
        x_buf[v, top:, :LANE] = part.astype(BF)
        x_buf[v, top:, LANE:] = places
    band_blocks(rtab, rtap_ref, False)
    band_blocks(ctab, ctap_ref, True)
    rband[...] = jnp.zeros_like(rband)
    cband[...] = jnp.zeros_like(cband)

    stores = []
    for b in range(blocks):
        k = kidx_ref[b]
        put_band(rband, rtab.at[k], 0, 0)
        put_band(cband, ctab.at[k], 0, 0)
        weight = lane_weights(ivt, b, width)
        loads[b].wait()
        if b + AHEAD < blocks:
            loads[b + AHEAD].start()
        mid = jnp.dot(rband[...], image[b], preferred_element_type=F32).astype(BF)
        mids[b] = mid[:, LANE:]
        stores.append(pltpu.make_async_copy(mids.at[b], mid_ref.at[b], mid_sem.at[b]))
        stores[-1].start()
        matched = jnp.dot(mid[:, : 3 * LANE], cband[...], preferred_element_type=F32)
        weighted = (matched * weight).astype(BF)
        for v in range(VISITS):
            x_buf[v, b * rows : (b + 1) * rows] = weighted[v * rows : (v + 1) * rows]
        if (b + 1) % GROUP == 0 or b + 1 == blocks:
            g = b // GROUP
            first = g * GROUP * rows
            last = (b + 1) * rows + (SUB if b + 1 == blocks else 0)
            part = pl.ds(first, last - first)
            stores.append(pltpu.make_async_copy(x_buf.at[:, part], x_ref.at[:, part], x_sem.at[g]))
            stores[-1].start()
    for store in stores:
        store.wait()


def match_y_kernel(kidx_ref, dest_ref, pos_ref, ctap_ref, iv_ref, mid_ref, *rest):
    n = len(Y_OFFSETS)
    y_refs = rest[:n]
    ctab, cband, ivt, mids, y_buf, whole, in_sem, y_sem = rest[n:]
    blocks, side = iv_ref.shape
    tiles, rows, width = side // LANE, side // VISITS, side // 2
    top = blocks * rows
    loads = [pltpu.make_async_copy(mid_ref.at[b], mids.at[b], in_sem.at[b]) for b in range(blocks)]
    for load in loads[:AHEAD]:
        load.start()

    places = combo_rows(dest_ref, pos_ref, blocks)
    ivt[...] = jnp.transpose(padded_weights(iv_ref)).astype(BF)
    for i in range(n):
        y_buf[i, top:, :LANE] = places
        y_buf[i, top:, LANE:] = places
    band_blocks(ctab, ctap_ref, True)
    cband[...] = jnp.zeros_like(cband)

    mc, my = lax.axis_index("core"), lax.axis_index("y")
    stores = []
    for b in range(blocks):
        put_band(cband, ctab.at[kidx_ref[b]], tiles - 3, tiles // 2)
        weight = lane_weights(ivt, b, width)
        loads[b].wait()
        if b + AHEAD < blocks:
            loads[b + AHEAD].start()
        matched = jnp.dot(mids[b], cband[...], preferred_element_type=F32)
        whole[b % 2] = (matched * weight).astype(BF)
        for i, (dc, dy) in enumerate(Y_OFFSETS):
            core, sub = lax.rem(mc + dc, NC), lax.rem(my + dy, NY)
            for x in range(NX):
                start = pl.multiple_of((x * NC + core) * rows + sub * SUB, SUB)
                y_buf[i, b * rows + x * SUB : b * rows + (x + 1) * SUB] = whole[b % 2, pl.ds(start, SUB), :]
        if (b + 1) % GROUP == 0 or b + 1 == blocks:
            g = b // GROUP
            first = g * GROUP * rows
            last = (b + 1) * rows + (SUB if b + 1 == blocks else 0)
            part = pl.ds(first, last - first)
            for i in range(n):
                stores.append(pltpu.make_async_copy(y_buf.at[i, part], y_refs[i].at[part], y_sem.at[g, i]))
                stores[-1].start()
    for store in stores:
        store.wait()


def match(kidx, dest, position, row_taps, col_taps, image, inv_var):
    blocks, side, _ = image.shape
    rows, width = side // VISITS, side // 2
    tall = blocks * rows + SUB
    groups = -(-blocks // GROUP)
    n = len(Y_OFFSETS)
    smem = pl.BlockSpec(memory_space=pltpu.SMEM)
    vmem = pl.BlockSpec(memory_space=pltpu.VMEM)
    hbm = pl.BlockSpec(memory_space=pltpu.HBM)
    table = pltpu.VMEM((NB, LANE, 3 * LANE), BF)
    band = pltpu.VMEM((3 * LANE, width), BF)
    turned = pltpu.VMEM((side, LANE), BF)
    sems = pltpu.SemaphoreType.DMA
    shape = jax.ShapeDtypeStruct
    rest = (blocks, side, side - LANE)
    params = pltpu.CompilerParams(vmem_limit_bytes=VMEM_BIG)
    cost = pl.CostEstimate(flops=WORK, bytes_accessed=image.size * 4, transcendentals=0)
    x_part, mid = pl.pallas_call(
        match_x_kernel,
        in_specs=[smem] * 3 + [vmem] * 3 + [hbm],
        out_specs=[hbm] * 2,
        out_shape=[shape((VISITS, tall, width), BF), shape(rest, BF)],
        scratch_shapes=[
            table,
            table,
            pltpu.VMEM((side, side), BF),
            band,
            turned,
            pltpu.VMEM(image.shape, BF),
            pltpu.VMEM(rest, BF),
            pltpu.VMEM((VISITS, tall, width), BF),
            sems((blocks,)),
            sems((blocks,)),
            sems((groups,)),
        ],
        compiler_params=params,
        cost_estimate=cost,
        name="match_x",
    )(kidx, dest, position, row_taps, col_taps, inv_var, image)
    y_parts = pl.pallas_call(
        match_y_kernel,
        in_specs=[smem] * 3 + [vmem] * 2 + [hbm],
        out_specs=[hbm] * n,
        out_shape=[shape((tall, width), BF)] * n,
        scratch_shapes=[
            table,
            band,
            turned,
            pltpu.VMEM(rest, BF),
            pltpu.VMEM((n, tall, width), BF),
            pltpu.VMEM((2, side, width), BF),
            sems((blocks,)),
            sems((groups, n)),
        ],
        compiler_params=params,
        cost_estimate=cost,
        name="match_y",
    )(kidx, dest, position, col_taps, inv_var, mid)
    return x_part, y_parts


def read_places(notes, flat, smem, sem):
    places = jnp.concatenate([n.astype(F32) for n in notes], axis=0)
    size = VISITS * SUB
    row = lax.broadcasted_iota(jnp.int32, (size, LANE), 0)
    lane = lax.broadcasted_iota(jnp.int32, (size, LANE), 1)
    line = jnp.sum(jnp.where(row == lane, places, 0.0), axis=0, keepdims=True)
    flat[...] = line.astype(jnp.int32)
    copy = pltpu.make_async_copy(flat, smem, sem)
    copy.start()
    copy.wait()
    return line


def gather_x_kernel(in_ref, out_ref, done_ref, acc, flat, smem, sem):
    rows, width = acc.shape[1:]
    blocks = (in_ref.shape[1] - SUB) // rows
    top = blocks * rows
    done_ref[...] = jnp.zeros_like(done_ref)
    line = read_places([in_ref[v, top:, LANE:] for v in range(VISITS)], flat, smem, sem)
    acc[...] = jnp.zeros_like(acc)
    for v in range(VISITS):
        for b in range(blocks):
            acc[smem[0, v * SUB + b]] += in_ref[v, b * rows : (b + 1) * rows].astype(F32)
    place = lax.broadcasted_iota(jnp.int32, (COUNT, LANE), 0)
    hit = (place == line.astype(jnp.int32)).astype(F32).astype(BF)
    weights = jnp.concatenate([in_ref[v, top:, :LANE].astype(F32) for v in range(VISITS)], axis=0).astype(BF)
    den = jnp.dot(hit, weights, preferred_element_type=F32)
    high = den.astype(BF).astype(F32)
    both = jnp.concatenate([high, den - high], axis=1)
    for t in range(TILES):
        for p in range(POS):
            out_ref[t, p * rows : (p + 1) * rows] = acc[t * POS + p].astype(BF)
        pad = jnp.zeros((SUB - POS, width), F32)
        out_ref[t, POS * rows :] = jnp.concatenate([both[t * POS : (t + 1) * POS], pad], axis=0).astype(BF)


def gather_y_kernel(*rest):
    n = len(Y_OFFSETS)
    pieces, outs, (acc, flat, smem, sem, out_buf, out_sem) = rest[:n], rest[n + 1 : -6], rest[-6:]
    rows = acc.shape[1]
    blocks = (pieces[0].shape[0] - SUB) // rows
    mx = lax.axis_index("x")
    read_places([r[blocks * rows :, LANE:] for r in pieces], flat, smem, sem)
    acc[...] = jnp.zeros_like(acc)
    for i in range(n):
        for b in range(blocks):
            acc[smem[0, i * SUB + b]] += pieces[i][b * rows : (b + 1) * rows].astype(F32)
    stores = [pltpu.make_async_copy(out_buf.at[i], outs[i], out_sem.at[i]) for i in range(NX)]
    for i in range(NX):
        to = pl.multiple_of(lax.rem(mx + i, NX) * SUB, SUB)
        out_buf[i] = acc[:, pl.ds(to, SUB), :].astype(BF)
        stores[i].start()
    for store in stores:
        store.wait()


def vmem_call(kernel, name, out_shape, args, scratch=(), after=0, flops=0, hbm_out=False):
    hbm_out = hbm_out or jax.tree.map(lambda _: False, out_shape)
    vm = pl.BlockSpec(memory_space=pltpu.VMEM)
    anywhere = pl.BlockSpec(memory_space=pl.ANY)
    size = sum(a.size * a.dtype.itemsize for a in args)
    flops = flops or size
    return pl.pallas_call(
        kernel,
        in_specs=[vm] * (len(args) - after) + [anywhere] * after,
        out_specs=jax.tree.map(lambda far: pl.BlockSpec(memory_space=pltpu.HBM) if far else vm, hbm_out),
        out_shape=out_shape,
        scratch_shapes=list(scratch),
        compiler_params=pltpu.CompilerParams(vmem_limit_bytes=32 << 20),
        cost_estimate=pl.CostEstimate(flops=flops, bytes_accessed=2 * size, transcendentals=0),
        name=name,
    )(*args)


def ring_z_kernel(*refs):
    ins, outs = refs[:NX], refs[NX:]
    mz = lax.axis_index("z")
    for i in range(NZ):
        for y in range(NY):
            at = pl.ds((y * NZ + lax.rem(mz + i, NZ)) * POS, POS)
            outs[i][y] = sum(r[at].astype(F32) for r in ins).astype(BF)


def ring_y_kernel(*refs):
    ins, outs = refs[:NZ], refs[NZ:]
    my = lax.axis_index("y")
    for i in range(NY):
        at = lax.rem(my + i, NY)
        outs[i][...] = sum(r[at].astype(F32) for r in ins)


def finish_kernel(x_ref, *rest):
    y_refs, out_ref, inv = rest[:-2], rest[-2], rest[-1]
    rows = out_ref.shape[1]
    width = x_ref.shape[2]
    my = lax.axis_index("y")
    notes = sum(x_ref[s, POS * rows :].astype(F32) for s in range(TILES))
    den = 1.0 / jnp.maximum(notes[:, :LANE] + notes[:, LANE:], 1.0)
    for p in range(POS):
        turned = jnp.transpose(jnp.broadcast_to(den[p : p + 1], (LANE, LANE)))[:rows]
        inv[p] = turned
        total = x_ref[0, p * rows : (p + 1) * rows].astype(F32)
        for s in range(1, TILES):
            total += x_ref[s, p * rows : (p + 1) * rows].astype(F32)
        for j in range(width // LANE):
            out_ref[p, :, j * LANE : (j + 1) * LANE] = total[:, j * LANE : (j + 1) * LANE] * turned
    for i, step in enumerate((0,) + RING_ORDER):
        at = pl.ds(pl.multiple_of(lax.rem(my - step + NY, NY) * SUB, SUB), SUB)
        for p in range(POS):
            scale = inv[p, at, :]
            for j in range(width // LANE):
                lanes = slice(width + j * LANE, width + (j + 1) * LANE)
                out_ref[p, at, lanes] = y_refs[i][p, :, j * LANE : (j + 1) * LANE] * scale


def ring(pieces, axis, size):
    out = [pieces[0]]
    for i in RING_ORDER:
        out.append(lax.ppermute(pieces[i], axis, [(s, (s + i) % size) for s in range(size)]))
    return out


def per_device(image, inv_var, kernel_index, dest, position, row_taps, col_taps):
    _, side, _ = image.shape
    rows, width = side // VISITS, side // 2
    shape = jax.ShapeDtypeStruct
    x_part, y_parts = match(kernel_index, dest[:, 0], position, row_taps, col_taps, image, inv_var)

    arrived = [y_parts[0]]
    for i in range(1, len(Y_OFFSETS)):
        dc, dy = Y_OFFSETS[i]
        perm = [
            (c * NY + y, ((c + dc) % NC) * NY + (y + dy) % NY) for c in range(NC) for y in range(NY)
        ]
        arrived.append(lax.ppermute(y_parts[i], ("core", "y"), perm))
    x_in = lax.all_to_all(x_part, ("x", "core"), 0, 0, tiled=True)

    scratch = [
        pltpu.VMEM((COUNT, rows, width), F32),
        pltpu.VMEM((1, LANE), jnp.int32),
        pltpu.SMEM((1, LANE), jnp.int32),
        pltpu.SemaphoreType.DMA,
    ]
    y_scratch = scratch + [pltpu.VMEM((NX, COUNT, SUB, width), BF), pltpu.SemaphoreType.DMA((NX,))]
    x_sum, x_done = vmem_call(
        gather_x_kernel, "gather_x", (shape((TILES, POS * rows + SUB, width), BF), shape((8, LANE), F32)), (x_in,), scratch, 0, GX
    )
    mine = vmem_call(gather_y_kernel, "gather_y", [shape((COUNT, SUB, width), BF)] * NX, (*arrived, x_done), y_scratch, 1, GY, [True] * NX)
    along_x = ring(mine, "x", NX)
    x_out = lax.all_to_all(x_sum, ("y", "z"), 0, 0, tiled=True)
    along_z = vmem_call(
        ring_z_kernel, "ring_z", [shape((NY, POS, SUB, width), BF)] * NZ, along_x, flops=RZ
    )
    along_z = ring(along_z, "z", NZ)
    along_y = vmem_call(ring_y_kernel, "ring_y", [shape((POS, SUB, width), F32)] * NY, along_z)
    along_y = ring(along_y, "y", NY)
    out = vmem_call(
        finish_kernel,
        "finish",
        shape((POS, rows, side), F32),
        (x_out, *along_y),
        [pltpu.VMEM((POS, rows, LANE), F32)],
    )
    return out[None]


def solution(mesh):
    mesh = Mesh(mesh.devices.reshape(NX, NC, NY, NZ), ("x", "core", "y", "z"))
    every = ("x", "core", "y", "z")
    in_specs = (P(every, None, None), P(every, None), P(every), P(every, None), P(every), P(), P())
    out_specs = P(("y", "z"), None, ("x", "core"), None)
    return jax.shard_map(
        per_device, mesh=mesh, in_specs=in_specs, out_specs=out_specs, check_vma=False
    )
```
